32 devices in a mesh: grp: 2 (over y), brick: 4 (over z), ray: 2 (over x), rep: 2 (over core).
Axes of the slice: x: 2, y: 2, z: 4, core: 2. Of those that a mesh axis runs over, the one named last changes fastest.
Arguments:
- samples: bfloat16 [32, 4, 16, 64], P(('grp', 'brick', 'ray', 'rep')), parts along dimension 0, may hold values from -6 to 6
- frequencies: float32 [16, 64], replicated, may hold values from -4 to 4
- w_first: bfloat16 [16, 128, 128], P('brick'), may hold values from -0.5 to 0.5
- w_second: bfloat16 [16, 128, 128], P('brick'), may hold values from -0.5 to 0.5
- w_out: bfloat16 [16, 4, 128], P('brick'), may hold values from -0.5 to 0.5
- brick_ids: int32 [32, 4], P(('grp', 'brick', 'ray', 'rep')), parts along dimension 0, may hold values from 0 to 15, as said below
- targets: float32 [3, 32], P(None, ('grp', 'brick', 'ray', 'rep')), parts along dimension 1, may hold values from -6 to 6
Outputs:
- prediction: float32 [3, 32], P(None, ('grp', 'brick', 'ray', 'rep')), parts along dimension 1
- grad_first: float32 [32, 128, 128], P(('grp', 'brick'), ('ray', 'rep')), parts along dimension 0
- grad_second: float32 [32, 128, 128], P(('grp', 'brick'), ('ray', 'rep')), parts along dimension 0
- grad_out: float32 [32, 4, 128], P(('grp', 'brick'), None, ('ray', 'rep')), parts along dimension 0
The draws below stay inside these ranges and needn't reach their ends.
There are 2 independent parts, one for each index of `grp`. The reference program is written for one: setup_inputs(seed, part) draws one part's arguments, and reference() takes and returns one part's arrays. A program takes and returns all parts, laid end to end along the dimension named above; an argument that names none is the same for every part. Nothing has to cross between parts.
Inputs may be any that keep to these rules, and one draw needn't show every extreme that they name: `brick_ids`: the owner of brick id is id // 4. Among the 4 blocks of each of the 1 rays of one device (an aligned block of rows), at most 2 name bricks of any one owner; 1 owners get exactly 2 blocks from every device.
All inputs are finite; a program needn't handle non-finite values.
Results may differ from the reference program's by a relative error of at most 0.0055.
Values may be sent and summed in bfloat16 or wider, within the bound.
A program may use at most 64 MiB of HBM per device.

```python
import jax
import jax.numpy as jnp
from jax import lax

S = 64
C_IN = 16
E = 128
H = 128
OUT = 4
SIG = 3
K = 4
CAP = 2
BR_DEV = 4
OWNERS = 4
HOT_OWNERS = 1
R_DEV = 1
RAYS = 16
BRICKS = 16


def draw_brick_ids(key, part):
    key = jax.random.fold_in(key, 7)
    owner_key, device_key = jax.random.split(key)
    owner_order = jax.random.permutation(owner_key, OWNERS)
    hot_slots = jnp.repeat(owner_order[:HOT_OWNERS], CAP)
    cold_slots = jnp.repeat(owner_order[HOT_OWNERS:], CAP)
    block_count = R_DEV * K

    def draw_device(single_random_key):
        pick_key, brick_key, shuffle_key = jax.random.split(single_random_key, 3)
        picked = jax.random.permutation(pick_key, cold_slots)[:block_count - HOT_OWNERS * CAP]
        owner_list = jax.random.permutation(shuffle_key, jnp.concatenate([hot_slots, picked]))
        local_ids = jax.random.randint(brick_key, (block_count,), 0, BR_DEV)
        return (owner_list * BR_DEV + local_ids).reshape(R_DEV, K)
    device_keys = jax.random.split(device_key, RAYS // R_DEV)
    return jax.vmap(draw_device)(device_keys).reshape(RAYS, K).astype(jnp.int32)


def shard_levels(rng, shape, pieces, low, high):
    loudness = 1.0
    for position, parts in pieces:
        steps = jax.random.uniform(jax.random.fold_in(jax.random.fold_in(rng, 6), position), (parts,), jnp.float32, low / len(pieces), high / len(pieces))
        loudness = loudness * jnp.repeat(jnp.exp(steps), shape[position] // parts).reshape((-1,) + (1,) * (len(shape) - 1 - position))
    return loudness


def noise(stream_key, shape, deviation, bound, shards=(), dtype=jnp.bfloat16):
    entries = jax.random.normal(stream_key, shape, jnp.float32) * deviation
    if len(shards) > 0:
        entries = shard_levels(stream_key, shape, shards, -0.22, 0.18) * entries
    return jnp.clip(entries, min=-bound, max=bound).astype(dtype)


def setup_inputs(seed: int = 0, part: int = 0) -> dict:
    key_of = jax.random.split(jax.random.key(seed), 8)
    part_splits = jax.random.split(jax.random.fold_in(key_of[7], part), 8)
    samples = noise(part_splits[0], (RAYS, K, C_IN, S), 1.0, 6.0, ((0, 16),))
    frequencies = noise(key_of[1], (C_IN, E // 2), 1.0, 4.0, (), jnp.float32)
    w_first = noise(key_of[2], (BRICKS, E, H), E ** -0.5, 0.5, ((0, 4),))
    w_second = noise(key_of[3], (BRICKS, H, H), H ** -0.5, 0.5, ((0, 4),))
    w_out = noise(key_of[4], (BRICKS, OUT, H), H ** -0.5, 0.5, ((0, 4),))
    brick_ids = draw_brick_ids(jax.random.fold_in(jax.random.fold_in(key_of[7], part), 71), part)
    targets = noise(part_splits[6], (SIG, RAYS), 1.0, 6.0, ((1, 16),), jnp.float32)
    return {"samples": samples, "frequencies": frequencies, "w_first": w_first, "w_second": w_second, "w_out": w_out, "brick_ids": brick_ids, "targets": targets}


loss_scale = 16.0

def silu_slope(values):
    squashed = jax.nn.sigmoid(values)
    return squashed * (1.0 + values * (1.0 - squashed))

def rounded(values):
    return lax.optimization_barrier(values.astype(jnp.bfloat16)).astype(jnp.float32)

def composite(field_rows):
    ray_rows = field_rows.shape[0]
    length = field_rows.shape[3]
    density = jax.nn.softplus(field_rows[:, :, 0, :]).reshape(ray_rows, -1)
    signal = jnp.moveaxis(field_rows[:, :, 1:, :], 2, 1).reshape(ray_rows, field_rows.shape[2] - 1, -1)
    optical = density * (1.0 / length)
    before = jnp.cumsum(optical, axis=1) - optical
    weights = jnp.exp(-before) * -jnp.expm1(-optical)
    return lax.optimization_barrier(jnp.sum(weights[:, None, :] * signal, axis=2)).T

def encode(blocks, frequencies):
    phases = jnp.einsum('gcn,cf->gnf', blocks.astype(jnp.float32), frequencies, precision=lax.Precision.HIGHEST)
    return jnp.concatenate([jnp.sin(phases), jnp.cos(phases)], axis=-1).astype(jnp.bfloat16)

def reference(samples, frequencies, w_first, w_second, w_out, brick_ids, targets):
    groups = RAYS // R_DEV
    highest = lax.Precision.HIGHEST
    scanned = (samples.reshape(groups, R_DEV * K, C_IN, S), brick_ids.reshape(groups, R_DEV * K), jnp.transpose(targets.reshape(SIG, groups, R_DEV), (1, 0, 2)))

    def step(carry, item):
        blocks, brick_of, target_rows = item
        encoded_features = encode(blocks, frequencies)
        first_layer = w_first[brick_of].astype(jnp.float32)
        second = w_second[brick_of].astype(jnp.float32)
        last = w_out[brick_of].astype(jnp.float32)
        first_preactivation = jnp.einsum('gne,geh->gnh', encoded_features.astype(jnp.float32), first_layer, precision=highest)
        hidden_first = rounded(jax.nn.silu(first_preactivation))
        pre_second = jnp.einsum('gnh,ghk->gnk', hidden_first, second, precision=highest)
        hidden_second = rounded(jax.nn.silu(pre_second))
        field = jnp.einsum('gnh,goh->gon', hidden_second, last, precision=highest)
        predicted, pullback = jax.vjp(composite, field.reshape(R_DEV, K, OUT, S))
        field_grad, = pullback(loss_scale * (predicted - target_rows))
        grad_rows = rounded(field_grad.reshape(R_DEV * K, OUT, S))
        slot_out = jnp.einsum('gon,gnh->goh', grad_rows, hidden_second, precision=highest)
        back_second = jnp.einsum('gon,goh->gnh', grad_rows, last, precision=highest)
        d_second = rounded(back_second * silu_slope(pre_second))
        slot_second = jnp.einsum('gnh,gnk->ghk', hidden_first, d_second, precision=highest)
        back_first = jnp.einsum('gnk,ghk->gnh', d_second, second, precision=highest)
        first_layer_delta = rounded(back_first * silu_slope(first_preactivation))
        first_layer_slot = jnp.einsum('gne,gnh->geh', encoded_features.astype(jnp.float32), first_layer_delta, precision=highest)
        totals = (carry[0] + jax.ops.segment_sum(first_layer_slot, brick_of, num_segments=BRICKS), carry[1] + jax.ops.segment_sum(slot_second, brick_of, num_segments=BRICKS), carry[2] + jax.ops.segment_sum(slot_out, brick_of, num_segments=BRICKS))
        return (totals, predicted)
    start = (jnp.zeros((BRICKS, E, H), jnp.float32), jnp.zeros((BRICKS, H, H), jnp.float32), jnp.zeros((BRICKS, OUT, H), jnp.float32))
    totals, predictions = lax.scan(step, start, scanned)
    prediction = jnp.transpose(predictions, (1, 0, 2)).reshape(SIG, RAYS)
    return (prediction, totals[0], totals[1], totals[2])
```

```python
import functools

import jax
import jax.numpy as jnp
from jax import lax
from jax.experimental import pallas as pl
from jax.experimental.pallas import tpu as pltpu
from jax.sharding import PartitionSpec as P

CAP = 2


loss_scale = 16.0


def silu_slope(values):
    squashed = jax.nn.sigmoid(values)
    return squashed * (1.0 + values * (1.0 - squashed))


def composite(field_rows):
    ray_rows = field_rows.shape[0]
    length = field_rows.shape[3]
    density = jax.nn.softplus(field_rows[:, :, 0, :]).reshape(ray_rows, -1)
    signal = jnp.moveaxis(field_rows[:, :, 1:, :], 2, 1).reshape(
        ray_rows, field_rows.shape[2] - 1, -1
    )
    optical = density * (1.0 / length)
    before = jnp.cumsum(optical, axis=1) - optical
    weights = jnp.exp(-before) * -jnp.expm1(-optical)
    return jnp.sum(weights[:, None, :] * signal, axis=2).T


def send_blocks(outgoing, labels):
    owners = lax.axis_size("brick")
    moved = (
        lax.all_to_all(
            outgoing.reshape((owners, CAP) + outgoing.shape[1:]),
            "brick",
            split_axis=0,
            concat_axis=0,
            tiled=True,
        ),
        lax.all_to_all(
            labels.reshape(owners, CAP), "brick", split_axis=0, concat_axis=0, tiled=True
        ),
    )
    return (moved[0].reshape(outgoing.shape), moved[1].reshape(labels.shape))


def trade_rows(rows_in):
    owners = lax.axis_size("brick")
    moved = lax.all_to_all(
        rows_in.reshape((owners, CAP) + rows_in.shape[1:]),
        "brick",
        split_axis=0,
        concat_axis=0,
        tiled=True,
    )
    return moved.reshape(rows_in.shape)


def per_brick(brick_table, slot_terms):
    summed = jnp.dot(
        brick_table.T, slot_terms.reshape(slot_terms.shape[0], -1), precision=lax.Precision.HIGHEST
    )
    return summed.reshape((brick_table.shape[1],) + slot_terms.shape[1:])


def layered_plan(samples, frequencies, w_first, w_second, w_out, brick_ids, targets):
    ray_rows, blocks_per_ray, channels, length = samples.shape
    bricks_here = w_first.shape[0]
    owners = lax.axis_size("brick")
    slot_total = owners * CAP
    block_count = ray_rows * blocks_per_ray
    flat_ids = brick_ids.reshape(block_count)
    owner_of = flat_ids // bricks_here
    local_id = flat_ids % bricks_here
    owner_table = (owner_of[:, None] == jnp.arange(owners, dtype=jnp.int32)[None, :]).astype(
        jnp.int32
    )
    earlier = jnp.cumsum(owner_table, axis=0) - owner_table
    incoming_rank = jnp.sum(earlier * owner_table, axis=1)
    slot_of = owner_of * CAP + incoming_rank
    outgoing = (
        jnp.zeros((slot_total, channels, length), jnp.bfloat16)
        .at[slot_of]
        .set(samples.reshape(block_count, channels, length))
    )
    labels = jnp.zeros((slot_total,), jnp.int32).at[slot_of].set(local_id)
    incoming, in_labels = send_blocks(outgoing, labels)
    phases = jnp.einsum(
        "scn,cf->snf", incoming.astype(jnp.float32), frequencies, precision=lax.Precision.HIGHEST
    )
    encoded_features = jnp.concatenate([jnp.sin(phases), jnp.cos(phases)], axis=-1).astype(
        jnp.bfloat16
    )
    first_layer = w_first[in_labels]
    second = w_second[in_labels]
    last = w_out[in_labels]
    first_preactivation = jnp.einsum(
        "kyd,kdc->kyc", encoded_features, first_layer, preferred_element_type=jnp.float32
    )
    hidden_first = jax.nn.silu(first_preactivation).astype(jnp.bfloat16)
    pre_second = jnp.einsum(
        "snh,shk->snk", hidden_first, second, preferred_element_type=jnp.float32
    )
    hidden_second = jax.nn.silu(pre_second).astype(jnp.bfloat16)
    field = jnp.einsum("snh,soh->son", hidden_second, last, preferred_element_type=jnp.float32)
    returned = trade_rows(field)
    own_fields = returned[slot_of].reshape(ray_rows, blocks_per_ray, field.shape[1], length)
    predicted, pullback = jax.vjp(composite, own_fields)
    (field_grad,) = pullback(loss_scale * (predicted - targets))
    grad_slots = (
        jnp.zeros((slot_total,) + field.shape[1:], jnp.float32)
        .at[slot_of]
        .set(field_grad.reshape((block_count,) + field.shape[1:]))
    )
    grad_rows = trade_rows(grad_slots).astype(jnp.bfloat16)
    slot_out = jnp.einsum(
        "son,snh->soh", grad_rows, hidden_second, preferred_element_type=jnp.float32
    )
    back_second = jnp.einsum("son,soh->snh", grad_rows, last, preferred_element_type=jnp.float32)
    d_second = (back_second * silu_slope(pre_second)).astype(jnp.bfloat16)
    slot_second = jnp.einsum(
        "snh,snk->shk", hidden_first, d_second, preferred_element_type=jnp.float32
    )
    back_first = jnp.einsum("snk,shk->snh", d_second, second, preferred_element_type=jnp.float32)
    first_layer_delta = (back_first * silu_slope(first_preactivation)).astype(jnp.bfloat16)
    first_layer_slot = jnp.einsum(
        "gmj,gmd->gjd", encoded_features, first_layer_delta, preferred_element_type=jnp.float32
    )
    brick_table = (in_labels[:, None] == jnp.arange(bricks_here, dtype=jnp.int32)[None, :]).astype(
        jnp.float32
    )
    grad_first = per_brick(brick_table, first_layer_slot)
    grad_second = per_brick(brick_table, slot_second)
    grad_last = per_brick(brick_table, slot_out)
    grad_first, grad_second, grad_last = lax.psum(
        (grad_first, grad_second, grad_last), ("ray", "rep")
    )
    group_index = lax.axis_index(("ray", "rep"))
    group_count = lax.axis_size(("ray", "rep"))
    wide_share = grad_first.shape[1] // group_count
    hidden_share = grad_second.shape[1] // group_count
    grad_first = lax.dynamic_slice_in_dim(grad_first, group_index * wide_share, wide_share, 1)
    grad_second = lax.dynamic_slice_in_dim(grad_second, group_index * hidden_share, hidden_share, 1)
    grad_last = lax.dynamic_slice_in_dim(grad_last, group_index * hidden_share, hidden_share, 2)
    return (predicted, grad_first, grad_second, grad_last)


F32 = jnp.float32
BF16 = jnp.bfloat16
MESH = pl.DeviceIdType.MESH


def split3(values):
    high = values.astype(BF16)
    rest = values - high.astype(F32)
    middle = rest.astype(BF16)
    low = (rest - middle.astype(F32)).astype(BF16)
    return high, middle, low


def nn(left, right):
    return jnp.dot(left, right, preferred_element_type=F32)


def nt(left, right):
    return lax.dot_general(left, right, (((1,), (1,)), ((), ())), preferred_element_type=F32)


def sin_cos(phases, half):
    turns = jnp.floor(phases * 0.3183098861837907 + (half + 0.5))
    shift = turns - half
    rest = phases - shift * 3.140625
    rest = rest - shift * 9.67502593994140625e-4
    rest = rest - shift * 1.509957990978376432e-7
    half_turns = turns * 0.5
    sign = 1.0 - 4.0 * (half_turns - jnp.floor(half_turns))
    square = rest * rest
    poly = -2.3889859e-08
    for factor in (2.7525562e-06, -0.00019840874, 0.0083333310, -0.16666667):
        poly = poly * square + factor
    return (rest + rest * square * poly) * sign


def softplus(values):
    decay = jnp.exp(-jnp.abs(values))
    ratio = decay / (2.0 + decay)
    square = ratio * ratio
    poly = jnp.full_like(values, 1.0 / 17.0)
    for order in (15, 13, 11, 9, 7, 5, 3, 1):
        poly = poly * square + 1.0 / order
    return jnp.maximum(values, 0.0) + 2.0 * ratio * poly


def one_minus_exp(values, decay):
    series = jnp.full_like(values, 1.0)
    for order in (8, 7, 6, 5, 4, 3, 2):
        series = 1.0 - values * (1.0 / order) * series
    return jnp.where(values < 0.5, values * series, 1.0 - decay)


def fused_kernel(
    owners,
    rays,
    reps,
    ids_ref,
    targets_ref,
    samples_ref,
    freq_ref,
    w1_ref,
    w2_ref,
    wo_ref,
    pred_ref,
    gf_ref,
    gs_ref,
    go_ref,
    sx,
    rx,
    sf,
    rf,
    sg,
    rg,
    enc_s,
    h1_s,
    h2_s,
    slope1_s,
    slope2_s,
    sx_send,
    sx_recv,
    relay_send,
    relay_recv,
    sf_send,
    sf_recv,
    sg_send,
    sg_recv,
):
    bricks, features, hidden = w1_ref.shape
    channels_out = wo_ref.shape[1]
    blocks, channels, length = samples_ref.shape[1:]
    groups = rays * reps
    wide = owners * CAP * length
    pair = CAP * length
    share = features // groups
    my_owner = lax.axis_index("brick")
    my_group = lax.axis_index("ray") * reps + lax.axis_index("rep")

    def device(owner_step, group_step):
        group = lax.rem(my_group + group_step, groups)
        return {
            "brick": lax.rem(my_owner + owner_step, owners),
            "ray": group // reps,
            "rep": lax.rem(group, reps),
        }

    barrier = pltpu.get_barrier_semaphore()
    for d in range(groups):
        for e in range(owners):
            if d or e:
                pl.semaphore_signal(barrier, inc=1, device_id=device(e, d), device_id_type=MESH)

    ids = [ids_ref[0, k] for k in range(blocks)]
    owner_of = [lax.div(i, bricks) for i in ids]
    local = [(ids[k] - owner_of[k] * bricks).astype(F32) for k in range(blocks)]
    rank = []
    for k in range(blocks):
        earlier = jnp.int32(0)
        for j in range(k):
            earlier = earlier + jnp.where(owner_of[j] == owner_of[k], 1, 0)
        rank.append(earlier)
    at_step = [lax.rem(my_owner + e, owners) for e in range(owners)]

    def chosen(k, e, c):
        return jnp.where(owner_of[k] == at_step[e], jnp.where(rank[k] == c, 1, 0), 0)

    picks = [
        [[chosen(k, e, c).astype(F32) for c in range(CAP)] for e in range(owners)]
        for k in range(blocks)
    ]
    tiles = [samples_ref[0, k].astype(F32) for k in range(blocks)]
    for e in range(owners):
        parts = []
        labels = []
        for c in range(CAP):
            block = jnp.zeros((channels, length), F32)
            label = jnp.float32(bricks)
            for k in range(blocks):
                block = block + picks[k][e][c] * tiles[k]
                label = label + picks[k][e][c] * (local[k] - bricks)
            parts.append(block)
            labels.append(jnp.full((16, length), label, F32))
        sx[e, :channels, :] = jnp.concatenate(parts, axis=1).astype(BF16)
        sx[e, channels:, :] = jnp.concatenate(labels, axis=1).astype(BF16)
    rx[0, 0] = sx[0]

    pl.semaphore_wait(barrier, owners * groups - 1)

    started = []
    first = []
    for e in range(1, owners):
        copy = pltpu.make_async_remote_copy(
            src_ref=sx.at[e],
            dst_ref=rx.at[0, e],
            send_sem=sx_send.at[e],
            recv_sem=sx_recv.at[e],
            device_id=device(e, 0),
            device_id_type=MESH,
        )
        copy.start()
        first.append(copy)

    freq = freq_ref[...]
    stacked = jnp.concatenate([part.astype(F32) for part in split3(freq)], axis=0)
    freq_t = jnp.concatenate([stacked, stacked], axis=1).T.astype(BF16)
    w1_t = jnp.concatenate(
        [w1_ref[b].astype(F32).T.astype(BF16) for b in range(bricks)], axis=1
    )
    w2_t = jnp.concatenate(
        [w2_ref[b].astype(F32).T.astype(BF16) for b in range(bricks)], axis=1
    )
    w2_cat = jnp.concatenate([w2_ref[b] for b in range(bricks)], axis=1)
    wo_rows = jnp.concatenate(
        [wo_ref[b].astype(F32) for b in range(bricks)], axis=0
    )
    wo_cat = wo_rows.astype(BF16)
    wo_t = wo_rows.T.astype(BF16)
    half = jnp.where(
        lax.broadcasted_iota(jnp.int32, (features, wide), 0) < features // 2, 0.0, 0.5
    ).astype(F32)
    brick_row = (
        lax.broadcasted_iota(jnp.int32, (bricks * channels_out, wide), 0) // channels_out
    ).astype(F32)

    for copy in first:
        copy.wait_recv()
        started.append(copy)
    relays = []
    for d in range(1, groups):
        copy = pltpu.make_async_remote_copy(
            src_ref=rx.at[0],
            dst_ref=rx.at[d],
            send_sem=relay_send.at[d],
            recv_sem=relay_recv.at[d],
            device_id=device(0, d),
            device_id_type=MESH,
        )
        copy.start()
        relays.append(copy)
        started.append(copy)

    def label_tile(d):
        return jnp.concatenate(
            [rx[d, e, channels:, :].astype(F32) for e in range(owners)], axis=1
        )

    def masks(d):
        labels = label_tile(d)
        return [jnp.where(labels == b, 1.0, 0.0).astype(BF16) for b in range(bricks)]

    def masked(values, mask):
        copies = values.shape[0] // 16
        return jnp.concatenate(
            [values * jnp.concatenate([m] * copies, axis=0) for m in mask], axis=0
        )

    def forward(d):
        mask = masks(d)
        rows = jnp.concatenate([rx[d, e, :channels, :] for e in range(owners)], axis=1)
        phases = nn(freq_t, jnp.concatenate([rows] * 3, axis=0))
        encoded = sin_cos(phases, half).astype(BF16)
        enc_s[d] = encoded
        pre = nn(w1_t, masked(encoded, mask))
        squashed = 1.0 / (1.0 + jnp.exp(-pre))
        value = pre * squashed
        h1 = value.astype(BF16)
        h1_s[d] = h1
        slope1_s[d] = squashed + value * (1.0 - squashed)
        pre = nn(w2_t, masked(h1, mask))
        squashed = 1.0 / (1.0 + jnp.exp(-pre))
        value = pre * squashed
        h2 = value.astype(BF16)
        h2_s[d] = h2
        slope2_s[d] = squashed + value * (1.0 - squashed)
        return h2

    h2 = forward(0)
    by_brick = nn(wo_cat, h2)
    labels = label_tile(0)
    field = jnp.zeros((channels_out, wide), F32)
    for b in range(bricks):
        rows = by_brick[b * channels_out : (b + 1) * channels_out]
        field = field + jnp.where(labels[:channels_out] == b, rows, 0.0)
    field = jnp.concatenate([field, jnp.zeros((8 - channels_out, wide), F32)], axis=0)
    for e in range(owners):
        sf[e] = field[:, e * pair : (e + 1) * pair]
    rf[0] = sf[0]
    fields = []
    for e in range(1, owners):
        copy = pltpu.make_async_remote_copy(
            src_ref=sf.at[e],
            dst_ref=rf.at[e],
            send_sem=sf_send.at[e],
            recv_sem=sf_recv.at[e],
            device_id=device(owners - e, 0),
            device_id_type=MESH,
        )
        copy.start()
        fields.append(copy)
        started.append(copy)

    for d in range(1, groups):
        relays[d - 1].wait_recv()
        forward(d)

    for copy in fields:
        copy.wait_recv()

    lane = lax.broadcasted_iota(jnp.int32, (8, pair), 1)
    got = [rf[e] for e in range(owners)]
    swapped = [
        jnp.concatenate([piece[:, length:], piece[:, :length]], axis=1) for piece in got
    ]
    pairs = []
    for p in range(blocks // CAP):
        halves = []
        for c in range(CAP):
            k = p * CAP + c
            total = jnp.zeros((8, pair), F32)
            for e in range(owners):
                total = total + picks[k][e][c] * got[e] + picks[k][e][1 - c] * swapped[e]
            halves.append(total)
        pairs.append(jnp.where(lane < length, halves[0], halves[1]))
    rows = len(pairs)
    channel = [
        jnp.concatenate([one[o : o + 1] for one in pairs], axis=0) for o in range(channels_out)
    ]
    row_of = lax.broadcasted_iota(jnp.int32, (pair, pair), 0)
    column_of = lax.broadcasted_iota(jnp.int32, (pair, pair), 1)
    upper = jnp.where(row_of < column_of, 1.0, 0.0).astype(BF16)
    lower = jnp.where(row_of > column_of, 1.0, 0.0).astype(BF16)

    def summed(values, triangle):
        high, middle, low = split3(values)
        return nn(high, triangle) + nn(middle, triangle) + nn(low, triangle)

    def offsets(values, reverse):
        totals = jnp.sum(values, axis=1, keepdims=True)
        kept = [jnp.zeros((1, 1), F32)]
        order = range(rows - 1, 0, -1) if reverse else range(rows - 1)
        for r in order:
            kept.append(kept[-1] + totals[r : r + 1])
        return jnp.concatenate(kept[::-1] if reverse else kept, axis=0)

    optical = softplus(channel[0]) * (1.0 / length)
    before = summed(optical, upper) + offsets(optical, False)
    through = jnp.exp(-before)
    decay = jnp.exp(-optical)
    weights = through * one_minus_exp(optical, decay)
    pull = []
    lifted = jnp.zeros((rows, pair), F32)
    for c in range(channels_out - 1):
        signal = channel[c + 1]
        predicted = jnp.sum(
            jnp.sum(weights * signal, axis=1, keepdims=True), axis=0, keepdims=True
        )
        pred_ref[c : c + 1, :] = predicted
        miss = loss_scale * (predicted - targets_ref[c, 0])
        pull.append(miss * weights)
        lifted = lifted + miss * signal
    product = lifted * weights
    after = summed(product, lower) + offsets(product, True)
    density_grad = (
        (lifted * through * decay - after) * (1.0 / length) / (1.0 + jnp.exp(-channel[0]))
    )
    grads = [density_grad] + pull
    grad_pairs = []
    for p in range(rows):
        rows4 = jnp.concatenate([g[p : p + 1] for g in grads], axis=0)
        grad_pairs.append(jnp.concatenate([rows4] * (8 // channels_out), axis=0))
    grad_swapped = [
        jnp.concatenate([piece[:, length:], piece[:, :length]], axis=1) for piece in grad_pairs
    ]
    for e in range(owners):
        halves = []
        for c in range(CAP):
            total = jnp.zeros((8, pair), F32)
            for k in range(blocks):
                source = grad_pairs if k % CAP == c else grad_swapped
                total = total + picks[k][e][c] * source[k // CAP]
            halves.append(total)
        tile = jnp.where(lane < length, halves[0], halves[1])
        sg[e] = jnp.concatenate([tile, tile], axis=0).astype(BF16)
    rg[0, 0] = sg[0]
    arriving = [[] for _ in range(groups)]
    for d in range(groups):
        for e in range(owners):
            if d or e:
                copy = pltpu.make_async_remote_copy(
                    src_ref=sg.at[e],
                    dst_ref=rg.at[d, e],
                    send_sem=sg_send.at[d, e],
                    recv_sem=sg_recv.at[d, e],
                    device_id=device(e, d),
                    device_id_type=MESH,
                )
                copy.start()
                arriving[d].append(copy)
                started.append(copy)

    mine = pl.ds(pl.multiple_of(my_group * share, share), share)
    gf = jnp.zeros((bricks * share, hidden), F32)
    gs = jnp.zeros((bricks * share, hidden), F32)
    go = jnp.zeros((bricks * channels_out, share), F32)
    for d in range(groups):
        mask = masks(d)
        for copy in arriving[d]:
            copy.wait_recv()
        rows16 = jnp.concatenate([rg[d, e] for e in range(owners)], axis=1)
        rows16 = rows16 * jnp.where(label_tile(d) == brick_row, 1.0, 0.0).astype(BF16)
        d2 = (nn(wo_t, rows16) * slope2_s[d]).astype(BF16)
        d1 = (nn(w2_cat, masked(d2, mask)) * slope1_s[d]).astype(BF16)
        gs = gs + nt(masked(h1_s[d, mine, :], mask), d2)
        go = go + nt(rows16, h2_s[d, mine, :])
        gf = gf + nt(masked(enc_s[d, mine, :], mask), d1)
    for b in range(bricks):
        gf_ref[b] = gf[b * share : (b + 1) * share]
        gs_ref[b] = gs[b * share : (b + 1) * share]
        go_ref[b] = go[b * channels_out : (b + 1) * channels_out]

    for copy in started:
        copy.wait_send()


def fused_plan(samples, frequencies, w_first, w_second, w_out, brick_ids, targets):
    owners = lax.axis_size("brick")
    rays = lax.axis_size("ray")
    reps = lax.axis_size("rep")
    groups = rays * reps
    bricks, features, hidden = w_first.shape
    out = w_out.shape[1]
    length = samples.shape[3]
    pair = CAP * length
    wide = owners * pair
    share = features // groups
    vmem = pl.BlockSpec(memory_space=pltpu.VMEM)
    smem = pl.BlockSpec(memory_space=pltpu.SMEM)
    dma = pltpu.SemaphoreType.DMA
    return pl.pallas_call(
        functools.partial(fused_kernel, owners, rays, reps),
        out_shape=(
            jax.ShapeDtypeStruct(targets.shape, F32),
            jax.ShapeDtypeStruct((bricks, share, hidden), F32),
            jax.ShapeDtypeStruct((bricks, share, hidden), F32),
            jax.ShapeDtypeStruct((bricks, out, share), F32),
        ),
        in_specs=[smem, smem, vmem, vmem, vmem, vmem, vmem],
        out_specs=(vmem, vmem, vmem, vmem),
        scratch_shapes=[
            pltpu.VMEM((owners, 32, pair), BF16),
            pltpu.VMEM((groups, owners, 32, pair), BF16),
            pltpu.VMEM((owners, 8, pair), F32),
            pltpu.VMEM((owners, 8, pair), F32),
            pltpu.VMEM((owners, 16, pair), BF16),
            pltpu.VMEM((groups, owners, 16, pair), BF16),
            pltpu.VMEM((groups, features, wide), BF16),
            pltpu.VMEM((groups, hidden, wide), BF16),
            pltpu.VMEM((groups, hidden, wide), BF16),
            pltpu.VMEM((groups, hidden, wide), F32),
            pltpu.VMEM((groups, hidden, wide), F32),
            dma((owners,)),
            dma((owners,)),
            dma((groups,)),
            dma((groups,)),
            dma((owners,)),
            dma((owners,)),
            dma((groups, owners)),
            dma((groups, owners)),
        ],
        compiler_params=pltpu.CompilerParams(
            collective_id=0, has_side_effects=True, vmem_limit_bytes=40 * 1024 * 1024
        ),
    )(brick_ids, targets, samples, frequencies, w_first, w_second, w_out)


def on_device(samples, frequencies, w_first, w_second, w_out, brick_ids, targets):
    owners = lax.axis_size("brick")
    groups = lax.axis_size(("ray", "rep"))
    bricks, features, hidden = w_first.shape
    ray_rows, blocks, channels, length = samples.shape
    fits = (
        ray_rows == 1
        and blocks % CAP == 0
        and CAP == 2
        and CAP * length == 128
        and channels == 16
        and bricks * w_out.shape[1] == 16
        and features == hidden
        and features % (16 * groups) == 0
        and groups * owners <= 16
    )
    plan = fused_plan if fits else layered_plan
    return plan(samples, frequencies, w_first, w_second, w_out, brick_ids, targets)


def solution(mesh):
    return jax.shard_map(
        on_device,
        mesh=mesh,
        in_specs=(
            P(("grp", "brick", "ray", "rep"), None, None, None),
            P(),
            P("brick", None, None),
            P("brick", None, None),
            P("brick", None, None),
            P(("grp", "brick", "ray", "rep"), None),
            P(None, ("grp", "brick", "ray", "rep")),
        ),
        out_specs=(
            P(None, ("grp", "brick", "ray", "rep")),
            P(("grp", "brick"), ("ray", "rep"), None),
            P(("grp", "brick"), ("ray", "rep"), None),
            P(("grp", "brick"), None, ("ray", "rep")),
        ),
        check_vma=False,
    )
```

```python
import functools

import jax
import jax.numpy as jnp
from jax import lax
from jax.experimental import pallas as pl
from jax.experimental.pallas import tpu as pltpu
from jax.sharding import PartitionSpec as P

CAP = 2


loss_scale = 16.0


def silu_slope(values):
    squashed = jax.nn.sigmoid(values)
    return squashed * (1.0 + values * (1.0 - squashed))


def composite(field_rows):
    ray_rows = field_rows.shape[0]
    length = field_rows.shape[3]
    density = jax.nn.softplus(field_rows[:, :, 0, :]).reshape(ray_rows, -1)
    signal = jnp.moveaxis(field_rows[:, :, 1:, :], 2, 1).reshape(
        ray_rows, field_rows.shape[2] - 1, -1
    )
    optical = density * (1.0 / length)
    before = jnp.cumsum(optical, axis=1) - optical
    weights = jnp.exp(-before) * -jnp.expm1(-optical)
    return jnp.sum(weights[:, None, :] * signal, axis=2).T


def send_blocks(outgoing, labels):
    owners = lax.axis_size("brick")
    moved = (
        lax.all_to_all(
            outgoing.reshape((owners, CAP) + outgoing.shape[1:]),
            "brick",
            split_axis=0,
            concat_axis=0,
            tiled=True,
        ),
        lax.all_to_all(
            labels.reshape(owners, CAP), "brick", split_axis=0, concat_axis=0, tiled=True
        ),
    )
    return (moved[0].reshape(outgoing.shape), moved[1].reshape(labels.shape))


def trade_rows(rows_in):
    owners = lax.axis_size("brick")
    moved = lax.all_to_all(
        rows_in.reshape((owners, CAP) + rows_in.shape[1:]),
        "brick",
        split_axis=0,
        concat_axis=0,
        tiled=True,
    )
    return moved.reshape(rows_in.shape)


def per_brick(brick_table, slot_terms):
    summed = jnp.dot(
        brick_table.T, slot_terms.reshape(slot_terms.shape[0], -1), precision=lax.Precision.HIGHEST
    )
    return summed.reshape((brick_table.shape[1],) + slot_terms.shape[1:])


def layered_plan(samples, frequencies, w_first, w_second, w_out, brick_ids, targets):
    ray_rows, blocks_per_ray, channels, length = samples.shape
    bricks_here = w_first.shape[0]
    owners = lax.axis_size("brick")
    slot_total = owners * CAP
    block_count = ray_rows * blocks_per_ray
    flat_ids = brick_ids.reshape(block_count)
    owner_of = flat_ids // bricks_here
    local_id = flat_ids % bricks_here
    owner_table = (owner_of[:, None] == jnp.arange(owners, dtype=jnp.int32)[None, :]).astype(
        jnp.int32
    )
    earlier = jnp.cumsum(owner_table, axis=0) - owner_table
    incoming_rank = jnp.sum(earlier * owner_table, axis=1)
    slot_of = owner_of * CAP + incoming_rank
    outgoing = (
        jnp.zeros((slot_total, channels, length), jnp.bfloat16)
        .at[slot_of]
        .set(samples.reshape(block_count, channels, length))
    )
    labels = jnp.zeros((slot_total,), jnp.int32).at[slot_of].set(local_id)
    incoming, in_labels = send_blocks(outgoing, labels)
    phases = jnp.einsum(
        "scn,cf->snf", incoming.astype(jnp.float32), frequencies, precision=lax.Precision.HIGHEST
    )
    encoded_features = jnp.concatenate([jnp.sin(phases), jnp.cos(phases)], axis=-1).astype(
        jnp.bfloat16
    )
    first_layer = w_first[in_labels]
    second = w_second[in_labels]
    last = w_out[in_labels]
    first_preactivation = jnp.einsum(
        "kyd,kdc->kyc", encoded_features, first_layer, preferred_element_type=jnp.float32
    )
    hidden_first = jax.nn.silu(first_preactivation).astype(jnp.bfloat16)
    pre_second = jnp.einsum(
        "snh,shk->snk", hidden_first, second, preferred_element_type=jnp.float32
    )
    hidden_second = jax.nn.silu(pre_second).astype(jnp.bfloat16)
    field = jnp.einsum("snh,soh->son", hidden_second, last, preferred_element_type=jnp.float32)
    returned = trade_rows(field)
    own_fields = returned[slot_of].reshape(ray_rows, blocks_per_ray, field.shape[1], length)
    predicted, pullback = jax.vjp(composite, own_fields)
    (field_grad,) = pullback(loss_scale * (predicted - targets))
    grad_slots = (
        jnp.zeros((slot_total,) + field.shape[1:], jnp.float32)
        .at[slot_of]
        .set(field_grad.reshape((block_count,) + field.shape[1:]))
    )
    grad_rows = trade_rows(grad_slots).astype(jnp.bfloat16)
    slot_out = jnp.einsum(
        "son,snh->soh", grad_rows, hidden_second, preferred_element_type=jnp.float32
    )
    back_second = jnp.einsum("son,soh->snh", grad_rows, last, preferred_element_type=jnp.float32)
    d_second = (back_second * silu_slope(pre_second)).astype(jnp.bfloat16)
    slot_second = jnp.einsum(
        "snh,snk->shk", hidden_first, d_second, preferred_element_type=jnp.float32
    )
    back_first = jnp.einsum("snk,shk->snh", d_second, second, preferred_element_type=jnp.float32)
    first_layer_delta = (back_first * silu_slope(first_preactivation)).astype(jnp.bfloat16)
    first_layer_slot = jnp.einsum(
        "gmj,gmd->gjd", encoded_features, first_layer_delta, preferred_element_type=jnp.float32
    )
    brick_table = (in_labels[:, None] == jnp.arange(bricks_here, dtype=jnp.int32)[None, :]).astype(
        jnp.float32
    )
    grad_first = per_brick(brick_table, first_layer_slot)
    grad_second = per_brick(brick_table, slot_second)
    grad_last = per_brick(brick_table, slot_out)
    grad_first, grad_second, grad_last = lax.psum(
        (grad_first, grad_second, grad_last), ("ray", "rep")
    )
    group_index = lax.axis_index(("ray", "rep"))
    group_count = lax.axis_size(("ray", "rep"))
    wide_share = grad_first.shape[1] // group_count
    hidden_share = grad_second.shape[1] // group_count
    grad_first = lax.dynamic_slice_in_dim(grad_first, group_index * wide_share, wide_share, 1)
    grad_second = lax.dynamic_slice_in_dim(grad_second, group_index * hidden_share, hidden_share, 1)
    grad_last = lax.dynamic_slice_in_dim(grad_last, group_index * hidden_share, hidden_share, 2)
    return (predicted, grad_first, grad_second, grad_last)


EARLY = 2
F32 = jnp.float32
BF16 = jnp.bfloat16
MESH = pl.DeviceIdType.MESH


def split3(values):
    high = values.astype(BF16)
    rest = values - high.astype(F32)
    middle = rest.astype(BF16)
    low = (rest - middle.astype(F32)).astype(BF16)
    return high, middle, low


def nn(left, right):
    return jnp.dot(left, right, preferred_element_type=F32)


def nt(left, right):
    return lax.dot_general(left, right, (((1,), (1,)), ((), ())), preferred_element_type=F32)


def sin_cos(phases, half):
    turns = jnp.floor(phases * 0.3183098861837907 + (half + 0.5))
    shift = turns - half
    rest = phases - shift * 3.140625
    rest = rest - shift * 9.67502593994140625e-4
    rest = rest - shift * 1.509957990978376432e-7
    half_turns = turns * 0.5
    sign = 1.0 - 4.0 * (half_turns - jnp.floor(half_turns))
    square = rest * rest
    poly = -2.3889859e-08
    for factor in (2.7525562e-06, -0.00019840874, 0.0083333310, -0.16666667):
        poly = poly * square + factor
    return (rest + rest * square * poly) * sign


def softplus(values):
    decay = jnp.exp(-jnp.abs(values))
    ratio = decay / (2.0 + decay)
    square = ratio * ratio
    poly = jnp.full_like(values, 1.0 / 17.0)
    for order in (15, 13, 11, 9, 7, 5, 3, 1):
        poly = poly * square + 1.0 / order
    return jnp.maximum(values, 0.0) + 2.0 * ratio * poly


def one_minus_exp(values, decay):
    series = jnp.full_like(values, 1.0)
    for order in (8, 7, 6, 5, 4, 3, 2):
        series = 1.0 - values * (1.0 / order) * series
    return jnp.where(values < 0.5, values * series, 1.0 - decay)


def fused_kernel(
    owners,
    rays,
    reps,
    ids_ref,
    targets_ref,
    samples_hbm,
    freq_hbm,
    w1_hbm,
    w2_hbm,
    wo_hbm,
    pred_ref,
    gf_ref,
    gs_ref,
    go_ref,
    sx,
    rx,
    sf,
    rf,
    sg,
    rg,
    samples_ref,
    freq_ref,
    w1_ref,
    w2_ref,
    wo_ref,
    enc_s,
    h1_s,
    h2_s,
    slope1_s,
    slope2_s,
    load_sem,
    sx_send,
    sx_recv,
    relay_send,
    relay_recv,
    sf_send,
    sf_recv,
    sg_send,
    sg_recv,
):
    bricks, features, hidden = w1_ref.shape
    channels_out = wo_ref.shape[1]
    blocks, channels, length = samples_ref.shape[1:]
    groups = rays * reps
    wide = owners * CAP * length
    pair = CAP * length
    share = features // groups
    my_owner = lax.axis_index("brick")
    my_group = lax.axis_index("ray") * reps + lax.axis_index("rep")

    def device(owner_step, group_step):
        group = lax.rem(my_group + group_step, groups)
        return {
            "brick": lax.rem(my_owner + owner_step, owners),
            "ray": group // reps,
            "rep": lax.rem(group, reps),
        }

    loads = [
        pltpu.make_async_copy(source, target, load_sem.at[i])
        for i, (source, target) in enumerate(
            (
                (samples_hbm, samples_ref),
                (freq_hbm, freq_ref),
                (w1_hbm, w1_ref),
                (w2_hbm, w2_ref),
                (wo_hbm, wo_ref),
            )
        )
    ]
    for load in loads:
        load.start()
    barrier = pltpu.get_barrier_semaphore()
    for d in range(groups):
        for e in range(owners):
            if d or e:
                pl.semaphore_signal(barrier, inc=1, device_id=device(e, d), device_id_type=MESH)

    ids = [ids_ref[0, k] for k in range(blocks)]
    owner_of = [lax.div(i, bricks) for i in ids]
    local = [(ids[k] - owner_of[k] * bricks).astype(F32) for k in range(blocks)]
    rank = []
    for k in range(blocks):
        earlier = jnp.int32(0)
        for j in range(k):
            earlier = earlier + jnp.where(owner_of[j] == owner_of[k], 1, 0)
        rank.append(earlier)
    at_step = [lax.rem(my_owner + e, owners) for e in range(owners)]

    def chosen(k, e, c):
        return jnp.where(owner_of[k] == at_step[e], jnp.where(rank[k] == c, 1, 0), 0)

    picks = [
        [[chosen(k, e, c).astype(F32) for c in range(CAP)] for e in range(owners)]
        for k in range(blocks)
    ]
    loads[0].wait()
    tiles = [samples_ref[0, k].astype(F32) for k in range(blocks)]
    for e in range(owners):
        parts = []
        labels = []
        for c in range(CAP):
            block = jnp.zeros((channels, length), F32)
            label = jnp.float32(bricks)
            for k in range(blocks):
                block = block + picks[k][e][c] * tiles[k]
                label = label + picks[k][e][c] * (local[k] - bricks)
            parts.append(block)
            labels.append(jnp.full((16, length), label, F32))
        sx[e, :channels, :] = jnp.concatenate(parts, axis=1).astype(BF16)
        sx[e, channels:, :] = jnp.concatenate(labels, axis=1).astype(BF16)
    rx[0, 0] = sx[0]

    pl.semaphore_wait(barrier, owners * groups - 1)

    started = []
    first = []
    for e in range(1, owners):
        copy = pltpu.make_async_remote_copy(
            src_ref=sx.at[e],
            dst_ref=rx.at[0, e],
            send_sem=sx_send.at[e],
            recv_sem=sx_recv.at[e],
            device_id=device(e, 0),
            device_id_type=MESH,
        )
        copy.start()
        first.append(copy)

    for load in loads[1:]:
        load.wait()
    freq = freq_ref[...]
    stacked = jnp.concatenate([part.astype(F32) for part in split3(freq)], axis=0)
    freq_t = jnp.concatenate([stacked, stacked], axis=1).T.astype(BF16)
    w1_t = jnp.concatenate(
        [w1_ref[b].astype(F32).T.astype(BF16) for b in range(bricks)], axis=1
    )
    w2_t = jnp.concatenate(
        [w2_ref[b].astype(F32).T.astype(BF16) for b in range(bricks)], axis=1
    )
    w2_cat = jnp.concatenate([w2_ref[b] for b in range(bricks)], axis=1)
    wo_rows = jnp.concatenate(
        [wo_ref[b].astype(F32) for b in range(bricks)], axis=0
    )
    wo_cat = wo_rows.astype(BF16)
    wo_t = wo_rows.T.astype(BF16)
    half = jnp.where(
        lax.broadcasted_iota(jnp.int32, (features, wide), 0) < features // 2, 0.0, 0.5
    ).astype(F32)
    brick_row = (
        lax.broadcasted_iota(jnp.int32, (bricks * channels_out, wide), 0) // channels_out
    ).astype(F32)

    for copy in first:
        copy.wait_recv()
        started.append(copy)
    relays = []
    for d in range(1, groups):
        copy = pltpu.make_async_remote_copy(
            src_ref=rx.at[0],
            dst_ref=rx.at[d],
            send_sem=relay_send.at[d],
            recv_sem=relay_recv.at[d],
            device_id=device(0, d),
            device_id_type=MESH,
        )
        copy.start()
        relays.append(copy)
        started.append(copy)

    def label_tile(d):
        return jnp.concatenate(
            [rx[d, e, channels:, :].astype(F32) for e in range(owners)], axis=1
        )

    def masks(d):
        labels = label_tile(d)
        return [jnp.where(labels == b, 1.0, 0.0).astype(BF16) for b in range(bricks)]

    def masked(values, mask):
        copies = values.shape[0] // 16
        return jnp.concatenate(
            [values * jnp.concatenate([m] * copies, axis=0) for m in mask], axis=0
        )

    def forward(d):
        mask = masks(d)
        rows = jnp.concatenate([rx[d, e, :channels, :] for e in range(owners)], axis=1)
        phases = nn(freq_t, jnp.concatenate([rows] * 3, axis=0))
        encoded = sin_cos(phases, half).astype(BF16)
        enc_s[d] = encoded
        pre = nn(w1_t, masked(encoded, mask))
        squashed = 0.5 + 0.5 * jnp.tanh(0.5 * pre)
        value = pre * squashed
        h1 = value.astype(BF16)
        h1_s[d] = h1
        slope1_s[d] = squashed + value * (1.0 - squashed)
        pre = nn(w2_t, masked(h1, mask))
        squashed = 0.5 + 0.5 * jnp.tanh(0.5 * pre)
        value = pre * squashed
        h2 = value.astype(BF16)
        h2_s[d] = h2
        slope2_s[d] = squashed + value * (1.0 - squashed)
        return h2

    h2 = forward(0)
    by_brick = nn(wo_cat, h2)
    labels = label_tile(0)
    field = jnp.zeros((channels_out, wide), F32)
    for b in range(bricks):
        rows = by_brick[b * channels_out : (b + 1) * channels_out]
        field = field + jnp.where(labels[:channels_out] == b, rows, 0.0)
    field = jnp.concatenate([field, jnp.zeros((8 - channels_out, wide), F32)], axis=0)
    for e in range(owners):
        sf[e] = field[:, e * pair : (e + 1) * pair]
    rf[0] = sf[0]
    fields = []
    for e in range(1, owners):
        copy = pltpu.make_async_remote_copy(
            src_ref=sf.at[e],
            dst_ref=rf.at[e],
            send_sem=sf_send.at[e],
            recv_sem=sf_recv.at[e],
            device_id=device(owners - e, 0),
            device_id_type=MESH,
        )
        copy.start()
        fields.append(copy)
        started.append(copy)

    for d in range(1, EARLY):
        relays[d - 1].wait_recv()
        forward(d)

    for copy in fields:
        copy.wait_recv()

    lane = lax.broadcasted_iota(jnp.int32, (8, pair), 1)
    got = [rf[e] for e in range(owners)]
    swapped = [
        jnp.concatenate([piece[:, length:], piece[:, :length]], axis=1) for piece in got
    ]
    pairs = []
    for p in range(blocks // CAP):
        halves = []
        for c in range(CAP):
            k = p * CAP + c
            total = jnp.zeros((8, pair), F32)
            for e in range(owners):
                total = total + picks[k][e][c] * got[e] + picks[k][e][1 - c] * swapped[e]
            halves.append(total)
        pairs.append(jnp.where(lane < length, halves[0], halves[1]))
    rows = len(pairs)
    channel = [
        jnp.concatenate([one[o : o + 1] for one in pairs], axis=0) for o in range(channels_out)
    ]
    row_of = lax.broadcasted_iota(jnp.int32, (pair, pair), 0)
    column_of = lax.broadcasted_iota(jnp.int32, (pair, pair), 1)
    upper = jnp.where(row_of < column_of, 1.0, 0.0).astype(BF16)
    lower = jnp.where(row_of > column_of, 1.0, 0.0).astype(BF16)

    def summed(values, triangle):
        high, middle, low = split3(values)
        return nn(high, triangle) + nn(middle, triangle) + nn(low, triangle)

    def offsets(values, reverse):
        totals = jnp.sum(values, axis=1, keepdims=True)
        kept = [jnp.zeros((1, 1), F32)]
        order = range(rows - 1, 0, -1) if reverse else range(rows - 1)
        for r in order:
            kept.append(kept[-1] + totals[r : r + 1])
        return jnp.concatenate(kept[::-1] if reverse else kept, axis=0)

    optical = softplus(channel[0]) * (1.0 / length)
    before = summed(optical, upper) + offsets(optical, False)
    through = jnp.exp(-before)
    decay = jnp.exp(-optical)
    weights = through * one_minus_exp(optical, decay)
    pull = []
    predictions = []
    lifted = jnp.zeros((rows, pair), F32)
    for c in range(channels_out - 1):
        signal = channel[c + 1]
        predicted = jnp.sum(
            jnp.sum(weights * signal, axis=1, keepdims=True), axis=0, keepdims=True
        )
        predictions.append(predicted)
        miss = loss_scale * (predicted - targets_ref[0, c])
        pull.append(miss * weights)
        lifted = lifted + miss * signal
    pred_ref[...] = jnp.concatenate(predictions, axis=1)
    product = lifted * weights
    after = summed(product, lower) + offsets(product, True)
    density_grad = (
        (lifted * through * decay - after) * (1.0 / length) / (1.0 + jnp.exp(-channel[0]))
    )
    grads = [density_grad] + pull
    grad_pairs = []
    for p in range(rows):
        rows4 = jnp.concatenate([g[p : p + 1] for g in grads], axis=0)
        grad_pairs.append(jnp.concatenate([rows4] * (8 // channels_out), axis=0))
    grad_swapped = [
        jnp.concatenate([piece[:, length:], piece[:, :length]], axis=1) for piece in grad_pairs
    ]
    for e in range(owners):
        halves = []
        for c in range(CAP):
            total = jnp.zeros((8, pair), F32)
            for k in range(blocks):
                source = grad_pairs if k % CAP == c else grad_swapped
                total = total + picks[k][e][c] * source[k // CAP]
            halves.append(total)
        tile = jnp.where(lane < length, halves[0], halves[1])
        sg[e] = jnp.concatenate([tile, tile], axis=0).astype(BF16)
    rg[0, 0] = sg[0]
    arriving = [[] for _ in range(groups)]
    for d in range(groups):
        for e in range(owners):
            if d or e:
                copy = pltpu.make_async_remote_copy(
                    src_ref=sg.at[e],
                    dst_ref=rg.at[d, e],
                    send_sem=sg_send.at[d, e],
                    recv_sem=sg_recv.at[d, e],
                    device_id=device(e, d),
                    device_id_type=MESH,
                )
                copy.start()
                arriving[d].append(copy)
                started.append(copy)

    for d in range(EARLY, groups):
        relays[d - 1].wait_recv()
        forward(d)

    mine = pl.ds(pl.multiple_of(my_group * share, share), share)
    gf = jnp.zeros((bricks * share, hidden), F32)
    gs = jnp.zeros((bricks * share, hidden), F32)
    go = jnp.zeros((bricks * channels_out, share), F32)
    for d in range(groups):
        mask = masks(d)
        for copy in arriving[d]:
            copy.wait_recv()
        rows16 = jnp.concatenate([rg[d, e] for e in range(owners)], axis=1)
        rows16 = rows16 * jnp.where(label_tile(d) == brick_row, 1.0, 0.0).astype(BF16)
        d2 = (nn(wo_t, rows16) * slope2_s[d]).astype(BF16)
        d1 = (nn(w2_cat, masked(d2, mask)) * slope1_s[d]).astype(BF16)
        gs = gs + nt(masked(h1_s[d, mine, :], mask), d2)
        go = go + nt(rows16, h2_s[d, mine, :])
        gf = gf + nt(masked(enc_s[d, mine, :], mask), d1)
    for b in range(bricks):
        gf_ref[b] = gf[b * share : (b + 1) * share]
        gs_ref[b] = gs[b * share : (b + 1) * share]
        go_ref[b] = go[b * channels_out : (b + 1) * channels_out]

    for copy in started:
        copy.wait_send()


def place_kernel(*refs):
    sources, targets, sem = refs[:4], refs[4:8], refs[8]
    copies = [
        pltpu.make_async_copy(source, target, sem.at[i])
        for i, (source, target) in enumerate(zip(sources, targets))
    ]
    for copy in copies:
        copy.start()
    for copy in copies:
        copy.wait()


def fused_plan(samples, frequencies, w_first, w_second, w_out, brick_ids, targets):
    owners = lax.axis_size("brick")
    rays = lax.axis_size("ray")
    reps = lax.axis_size("rep")
    groups = rays * reps
    bricks, features, hidden = w_first.shape
    out = w_out.shape[1]
    length = samples.shape[3]
    pair = CAP * length
    wide = owners * pair
    share = features // groups
    vmem = pl.BlockSpec(memory_space=pltpu.VMEM)
    smem = pl.BlockSpec(memory_space=pltpu.SMEM)
    hbm = pl.BlockSpec(memory_space=pltpu.MemorySpace.HBM)
    dma = pltpu.SemaphoreType.DMA
    results = pl.pallas_call(
        functools.partial(fused_kernel, owners, rays, reps),
        out_shape=(
            jax.ShapeDtypeStruct((1, targets.shape[0]), F32),
            jax.ShapeDtypeStruct((bricks, share, hidden), F32),
            jax.ShapeDtypeStruct((bricks, share, hidden), F32),
            jax.ShapeDtypeStruct((bricks, out, share), F32),
        ),
        in_specs=[smem, smem, hbm, hbm, hbm, hbm, hbm],
        out_specs=(vmem, vmem, vmem, vmem),
        scratch_shapes=[
            pltpu.VMEM((owners, 32, pair), BF16),
            pltpu.VMEM((groups, owners, 32, pair), BF16),
            pltpu.VMEM((owners, 8, pair), F32),
            pltpu.VMEM((owners, 8, pair), F32),
            pltpu.VMEM((owners, 16, pair), BF16),
            pltpu.VMEM((groups, owners, 16, pair), BF16),
            pltpu.VMEM(samples.shape, BF16),
            pltpu.VMEM(frequencies.shape, F32),
            pltpu.VMEM(w_first.shape, BF16),
            pltpu.VMEM(w_second.shape, BF16),
            pltpu.VMEM(w_out.shape, BF16),
            pltpu.VMEM((groups, features, wide), BF16),
            pltpu.VMEM((groups, hidden, wide), BF16),
            pltpu.VMEM((groups, hidden, wide), BF16),
            pltpu.VMEM((groups, hidden, wide), F32),
            pltpu.VMEM((groups, hidden, wide), F32),
            dma((5,)),
            dma((owners,)),
            dma((owners,)),
            dma((groups,)),
            dma((groups,)),
            dma((owners,)),
            dma((owners,)),
            dma((groups, owners)),
            dma((groups, owners)),
        ],
        compiler_params=pltpu.CompilerParams(
            collective_id=0, has_side_effects=True,
            vmem_limit_bytes=63 * 1024 * 1024,
        ),
    )(brick_ids, targets.T, samples, frequencies, w_first, w_second, w_out)
    predicted, grad_first, grad_second, grad_last = pl.pallas_call(
        place_kernel,
        out_shape=tuple(jax.ShapeDtypeStruct(r.shape, r.dtype) for r in results),
        in_specs=[hbm] * 4,
        out_specs=(hbm,) * 4,
        scratch_shapes=[dma((4,))],
        compiler_params=pltpu.CompilerParams(vmem_limit_bytes=63 * 1024 * 1024),
    )(*results)
    return predicted.T, grad_first, grad_second, grad_last


def on_device(samples, frequencies, w_first, w_second, w_out, brick_ids, targets):
    owners = lax.axis_size("brick")
    groups = lax.axis_size(("ray", "rep"))
    bricks, features, hidden = w_first.shape
    ray_rows, blocks, channels, length = samples.shape
    fits = (
        ray_rows == 1
        and blocks % CAP == 0
        and CAP == 2
        and CAP * length == 128
        and channels == 16
        and bricks * w_out.shape[1] == 16
        and features == hidden
        and features % (16 * groups) == 0
        and groups * owners <= 16
    )
    plan = fused_plan if fits else layered_plan
    return plan(samples, frequencies, w_first, w_second, w_out, brick_ids, targets)


def solution(mesh):
    return jax.shard_map(
        on_device,
        mesh=mesh,
        in_specs=(
            P(("grp", "brick", "ray", "rep"), None, None, None),
            P(),
            P("brick", None, None),
            P("brick", None, None),
            P("brick", None, None),
            P(("grp", "brick", "ray", "rep"), None),
            P(None, ("grp", "brick", "ray", "rep")),
        ),
        out_specs=(
            P(None, ("grp", "brick", "ray", "rep")),
            P(("grp", "brick"), ("ray", "rep"), None),
            P(("grp", "brick"), ("ray", "rep"), None),
            P(("grp", "brick"), None, ("ray", "rep")),
        ),
        check_vma=False,
    )
```

```python
import functools

import jax
import jax.numpy as jnp
from jax import lax
from jax.experimental import pallas as pl
from jax.experimental.pallas import tpu as pltpu
from jax.sharding import PartitionSpec as P

CAP = 2


loss_scale = 16.0


def silu_slope(values):
    squashed = jax.nn.sigmoid(values)
    return squashed * (1.0 + values * (1.0 - squashed))


def composite(field_rows):
    ray_rows = field_rows.shape[0]
    length = field_rows.shape[3]
    density = jax.nn.softplus(field_rows[:, :, 0, :]).reshape(ray_rows, -1)
    signal = jnp.moveaxis(field_rows[:, :, 1:, :], 2, 1).reshape(
        ray_rows, field_rows.shape[2] - 1, -1
    )
    optical = density * (1.0 / length)
    before = jnp.cumsum(optical, axis=1) - optical
    weights = jnp.exp(-before) * -jnp.expm1(-optical)
    return jnp.sum(weights[:, None, :] * signal, axis=2).T


def send_blocks(outgoing, labels):
    owners = lax.axis_size("brick")
    moved = (
        lax.all_to_all(
            outgoing.reshape((owners, CAP) + outgoing.shape[1:]),
            "brick",
            split_axis=0,
            concat_axis=0,
            tiled=True,
        ),
        lax.all_to_all(
            labels.reshape(owners, CAP), "brick", split_axis=0, concat_axis=0, tiled=True
        ),
    )
    return (moved[0].reshape(outgoing.shape), moved[1].reshape(labels.shape))


def trade_rows(rows_in):
    owners = lax.axis_size("brick")
    moved = lax.all_to_all(
        rows_in.reshape((owners, CAP) + rows_in.shape[1:]),
        "brick",
        split_axis=0,
        concat_axis=0,
        tiled=True,
    )
    return moved.reshape(rows_in.shape)


def per_brick(brick_table, slot_terms):
    summed = jnp.dot(
        brick_table.T, slot_terms.reshape(slot_terms.shape[0], -1), precision=lax.Precision.HIGHEST
    )
    return summed.reshape((brick_table.shape[1],) + slot_terms.shape[1:])


def layered_plan(samples, frequencies, w_first, w_second, w_out, brick_ids, targets):
    ray_rows, blocks_per_ray, channels, length = samples.shape
    bricks_here = w_first.shape[0]
    owners = lax.axis_size("brick")
    slot_total = owners * CAP
    block_count = ray_rows * blocks_per_ray
    flat_ids = brick_ids.reshape(block_count)
    owner_of = flat_ids // bricks_here
    local_id = flat_ids % bricks_here
    owner_table = (owner_of[:, None] == jnp.arange(owners, dtype=jnp.int32)[None, :]).astype(
        jnp.int32
    )
    earlier = jnp.cumsum(owner_table, axis=0) - owner_table
    incoming_rank = jnp.sum(earlier * owner_table, axis=1)
    slot_of = owner_of * CAP + incoming_rank
    outgoing = (
        jnp.zeros((slot_total, channels, length), jnp.bfloat16)
        .at[slot_of]
        .set(samples.reshape(block_count, channels, length))
    )
    labels = jnp.zeros((slot_total,), jnp.int32).at[slot_of].set(local_id)
    incoming, in_labels = send_blocks(outgoing, labels)
    phases = jnp.einsum(
        "scn,cf->snf", incoming.astype(jnp.float32), frequencies, precision=lax.Precision.HIGHEST
    )
    encoded_features = jnp.concatenate([jnp.sin(phases), jnp.cos(phases)], axis=-1).astype(
        jnp.bfloat16
    )
    first_layer = w_first[in_labels]
    second = w_second[in_labels]
    last = w_out[in_labels]
    first_preactivation = jnp.einsum(
        "kyd,kdc->kyc", encoded_features, first_layer, preferred_element_type=jnp.float32
    )
    hidden_first = jax.nn.silu(first_preactivation).astype(jnp.bfloat16)
    pre_second = jnp.einsum(
        "snh,shk->snk", hidden_first, second, preferred_element_type=jnp.float32
    )
    hidden_second = jax.nn.silu(pre_second).astype(jnp.bfloat16)
    field = jnp.einsum("snh,soh->son", hidden_second, last, preferred_element_type=jnp.float32)
    returned = trade_rows(field)
    own_fields = returned[slot_of].reshape(ray_rows, blocks_per_ray, field.shape[1], length)
    predicted, pullback = jax.vjp(composite, own_fields)
    (field_grad,) = pullback(loss_scale * (predicted - targets))
    grad_slots = (
        jnp.zeros((slot_total,) + field.shape[1:], jnp.float32)
        .at[slot_of]
        .set(field_grad.reshape((block_count,) + field.shape[1:]))
    )
    grad_rows = trade_rows(grad_slots).astype(jnp.bfloat16)
    slot_out = jnp.einsum(
        "son,snh->soh", grad_rows, hidden_second, preferred_element_type=jnp.float32
    )
    back_second = jnp.einsum("son,soh->snh", grad_rows, last, preferred_element_type=jnp.float32)
    d_second = (back_second * silu_slope(pre_second)).astype(jnp.bfloat16)
    slot_second = jnp.einsum(
        "snh,snk->shk", hidden_first, d_second, preferred_element_type=jnp.float32
    )
    back_first = jnp.einsum("snk,shk->snh", d_second, second, preferred_element_type=jnp.float32)
    first_layer_delta = (back_first * silu_slope(first_preactivation)).astype(jnp.bfloat16)
    first_layer_slot = jnp.einsum(
        "gmj,gmd->gjd", encoded_features, first_layer_delta, preferred_element_type=jnp.float32
    )
    brick_table = (in_labels[:, None] == jnp.arange(bricks_here, dtype=jnp.int32)[None, :]).astype(
        jnp.float32
    )
    grad_first = per_brick(brick_table, first_layer_slot)
    grad_second = per_brick(brick_table, slot_second)
    grad_last = per_brick(brick_table, slot_out)
    grad_first, grad_second, grad_last = lax.psum(
        (grad_first, grad_second, grad_last), ("ray", "rep")
    )
    group_index = lax.axis_index(("ray", "rep"))
    group_count = lax.axis_size(("ray", "rep"))
    wide_share = grad_first.shape[1] // group_count
    hidden_share = grad_second.shape[1] // group_count
    grad_first = lax.dynamic_slice_in_dim(grad_first, group_index * wide_share, wide_share, 1)
    grad_second = lax.dynamic_slice_in_dim(grad_second, group_index * hidden_share, hidden_share, 1)
    grad_last = lax.dynamic_slice_in_dim(grad_last, group_index * hidden_share, hidden_share, 2)
    return (predicted, grad_first, grad_second, grad_last)


EARLY = 2
F32 = jnp.float32
BF16 = jnp.bfloat16
MESH = pl.DeviceIdType.MESH


def split3(values):
    high = values.astype(BF16)
    rest = values - high.astype(F32)
    middle = rest.astype(BF16)
    low = (rest - middle.astype(F32)).astype(BF16)
    return high, middle, low


def nn(left, right):
    return jnp.dot(left, right, preferred_element_type=F32)


def nt(left, right):
    return lax.dot_general(left, right, (((1,), (1,)), ((), ())), preferred_element_type=F32)


def sin_cos(phases, half):
    turns = jnp.floor(phases * 0.3183098861837907 + (half + 0.5))
    shift = turns - half
    rest = phases - shift * 3.140625
    rest = rest - shift * 9.67502593994140625e-4
    rest = rest - shift * 1.509957990978376432e-7
    half_turns = turns * 0.5
    sign = 1.0 - 4.0 * (half_turns - jnp.floor(half_turns))
    square = rest * rest
    poly = -2.3889859e-08
    for factor in (2.7525562e-06, -0.00019840874, 0.0083333310, -0.16666667):
        poly = poly * square + factor
    return (rest + rest * square * poly) * sign


def softplus(values):
    decay = jnp.exp(-jnp.abs(values))
    ratio = decay / (2.0 + decay)
    square = ratio * ratio
    poly = jnp.full_like(values, 1.0 / 17.0)
    for order in (15, 13, 11, 9, 7, 5, 3, 1):
        poly = poly * square + 1.0 / order
    return jnp.maximum(values, 0.0) + 2.0 * ratio * poly


def one_minus_exp(values, decay):
    series = jnp.full_like(values, 1.0)
    for order in (8, 7, 6, 5, 4, 3, 2):
        series = 1.0 - values * (1.0 / order) * series
    return jnp.where(values < 0.5, values * series, 1.0 - decay)


def fused_kernel(
    owners,
    rays,
    reps,
    ids_ref,
    targets_ref,
    samples_hbm,
    freq_hbm,
    w1_hbm,
    w2_hbm,
    wo_hbm,
    packed_ref,
    sx,
    rx,
    sf,
    rf,
    sg,
    rg,
    samples_ref,
    freq_ref,
    w1_ref,
    w2_ref,
    wo_ref,
    enc_s,
    h1_s,
    h2_s,
    slope1_s,
    slope2_s,
    load_sem,
    sx_send,
    sx_recv,
    relay_send,
    relay_recv,
    sf_send,
    sf_recv,
    sg_send,
    sg_recv,
):
    bricks, features, hidden = w1_ref.shape
    channels_out = wo_ref.shape[1]
    blocks, channels, length = samples_ref.shape[1:]
    groups = rays * reps
    wide = owners * CAP * length
    pair = CAP * length
    share = features // groups
    my_owner = lax.axis_index("brick")
    my_group = lax.axis_index("ray") * reps + lax.axis_index("rep")

    def device(owner_step, group_step):
        group = lax.rem(my_group + group_step, groups)
        return {
            "brick": lax.rem(my_owner + owner_step, owners),
            "ray": group // reps,
            "rep": lax.rem(group, reps),
        }

    loads = [
        pltpu.make_async_copy(source, target, load_sem.at[i])
        for i, (source, target) in enumerate(
            (
                (samples_hbm, samples_ref),
                (freq_hbm, freq_ref),
                (w1_hbm, w1_ref),
                (w2_hbm, w2_ref),
                (wo_hbm, wo_ref),
            )
        )
    ]
    for load in loads:
        load.start()
    barrier = pltpu.get_barrier_semaphore()
    for d in range(groups):
        for e in range(owners):
            if d or e:
                pl.semaphore_signal(barrier, inc=1, device_id=device(e, d), device_id_type=MESH)

    ids = [ids_ref[0, k] for k in range(blocks)]
    owner_of = [lax.div(i, bricks) for i in ids]
    local = [(ids[k] - owner_of[k] * bricks).astype(F32) for k in range(blocks)]
    rank = []
    for k in range(blocks):
        earlier = jnp.int32(0)
        for j in range(k):
            earlier = earlier + jnp.where(owner_of[j] == owner_of[k], 1, 0)
        rank.append(earlier)
    at_step = [lax.rem(my_owner + e, owners) for e in range(owners)]

    def chosen(k, e, c):
        return jnp.where(owner_of[k] == at_step[e], jnp.where(rank[k] == c, 1, 0), 0)

    picks = [
        [[chosen(k, e, c).astype(F32) for c in range(CAP)] for e in range(owners)]
        for k in range(blocks)
    ]
    loads[0].wait()
    tiles = [samples_ref[0, k].astype(F32) for k in range(blocks)]
    for e in range(owners):
        parts = []
        labels = []
        for c in range(CAP):
            block = jnp.zeros((channels, length), F32)
            label = jnp.float32(bricks)
            for k in range(blocks):
                block = block + picks[k][e][c] * tiles[k]
                label = label + picks[k][e][c] * (local[k] - bricks)
            parts.append(block)
            labels.append(jnp.full((16, length), label, F32))
        sx[e, :channels, :] = jnp.concatenate(parts, axis=1).astype(BF16)
        sx[e, channels:, :] = jnp.concatenate(labels, axis=1).astype(BF16)
    rx[0, 0] = sx[0]

    pl.semaphore_wait(barrier, owners * groups - 1)

    started = []
    first = []
    for e in range(1, owners):
        copy = pltpu.make_async_remote_copy(
            src_ref=sx.at[e],
            dst_ref=rx.at[0, e],
            send_sem=sx_send.at[e],
            recv_sem=sx_recv.at[e],
            device_id=device(e, 0),
            device_id_type=MESH,
        )
        copy.start()
        first.append(copy)

    for load in loads[1:]:
        load.wait()
    freq = freq_ref[...]
    stacked = jnp.concatenate([part.astype(F32) for part in split3(freq)], axis=0)
    freq_t = jnp.concatenate([stacked, stacked], axis=1).T.astype(BF16)
    w1_t = jnp.concatenate(
        [w1_ref[b].astype(F32).T.astype(BF16) for b in range(bricks)], axis=1
    )
    w2_t = jnp.concatenate(
        [w2_ref[b].astype(F32).T.astype(BF16) for b in range(bricks)], axis=1
    )
    w2_cat = jnp.concatenate([w2_ref[b] for b in range(bricks)], axis=1)
    wo_rows = jnp.concatenate(
        [wo_ref[b].astype(F32) for b in range(bricks)], axis=0
    )
    wo_cat = wo_rows.astype(BF16)
    wo_t = wo_rows.T.astype(BF16)
    half = jnp.where(
        lax.broadcasted_iota(jnp.int32, (features, wide), 0) < features // 2, 0.0, 0.5
    ).astype(F32)
    brick_row = (
        lax.broadcasted_iota(jnp.int32, (bricks * channels_out, wide), 0) // channels_out
    ).astype(F32)

    for copy in first:
        copy.wait_recv()
        started.append(copy)
    relays = []
    for d in range(1, groups):
        copy = pltpu.make_async_remote_copy(
            src_ref=rx.at[0],
            dst_ref=rx.at[d],
            send_sem=relay_send.at[d],
            recv_sem=relay_recv.at[d],
            device_id=device(0, d),
            device_id_type=MESH,
        )
        copy.start()
        relays.append(copy)
        started.append(copy)

    def label_tile(d):
        return jnp.concatenate(
            [rx[d, e, channels:, :].astype(F32) for e in range(owners)], axis=1
        )

    def masks(d):
        labels = label_tile(d)
        return [jnp.where(labels == b, 1.0, 0.0).astype(BF16) for b in range(bricks)]

    def masked(values, mask):
        copies = values.shape[0] // 16
        return jnp.concatenate(
            [values * jnp.concatenate([m] * copies, axis=0) for m in mask], axis=0
        )

    def forward(d):
        mask = masks(d)
        rows = jnp.concatenate([rx[d, e, :channels, :] for e in range(owners)], axis=1)
        phases = nn(freq_t, jnp.concatenate([rows] * 3, axis=0))
        encoded = sin_cos(phases, half).astype(BF16)
        enc_s[d] = encoded
        pre = nn(w1_t, masked(encoded, mask))
        squashed = 0.5 + 0.5 * jnp.tanh(0.5 * pre)
        value = pre * squashed
        h1 = value.astype(BF16)
        h1_s[d] = h1
        slope1_s[d] = squashed + value * (1.0 - squashed)
        pre = nn(w2_t, masked(h1, mask))
        squashed = 0.5 + 0.5 * jnp.tanh(0.5 * pre)
        value = pre * squashed
        h2 = value.astype(BF16)
        h2_s[d] = h2
        slope2_s[d] = squashed + value * (1.0 - squashed)
        return h2

    h2 = forward(0)
    by_brick = nn(wo_cat, h2)
    labels = label_tile(0)
    field = jnp.zeros((channels_out, wide), F32)
    for b in range(bricks):
        rows = by_brick[b * channels_out : (b + 1) * channels_out]
        field = field + jnp.where(labels[:channels_out] == b, rows, 0.0)
    field = jnp.concatenate([field, jnp.zeros((8 - channels_out, wide), F32)], axis=0)
    for e in range(owners):
        sf[e] = field[:, e * pair : (e + 1) * pair]
    rf[0] = sf[0]
    fields = []
    for e in range(1, owners):
        copy = pltpu.make_async_remote_copy(
            src_ref=sf.at[e],
            dst_ref=rf.at[e],
            send_sem=sf_send.at[e],
            recv_sem=sf_recv.at[e],
            device_id=device(owners - e, 0),
            device_id_type=MESH,
        )
        copy.start()
        fields.append(copy)
        started.append(copy)

    for d in range(1, EARLY):
        relays[d - 1].wait_recv()
        forward(d)

    for copy in fields:
        copy.wait_recv()

    lane = lax.broadcasted_iota(jnp.int32, (8, pair), 1)
    got = [rf[e] for e in range(owners)]
    swapped = [
        jnp.concatenate([piece[:, length:], piece[:, :length]], axis=1) for piece in got
    ]
    pairs = []
    for p in range(blocks // CAP):
        halves = []
        for c in range(CAP):
            k = p * CAP + c
            total = jnp.zeros((8, pair), F32)
            for e in range(owners):
                total = total + picks[k][e][c] * got[e] + picks[k][e][1 - c] * swapped[e]
            halves.append(total)
        pairs.append(jnp.where(lane < length, halves[0], halves[1]))
    rows = len(pairs)
    channel = [
        jnp.concatenate([one[o : o + 1] for one in pairs], axis=0) for o in range(channels_out)
    ]
    row_of = lax.broadcasted_iota(jnp.int32, (pair, pair), 0)
    column_of = lax.broadcasted_iota(jnp.int32, (pair, pair), 1)
    upper = jnp.where(row_of < column_of, 1.0, 0.0).astype(BF16)
    lower = jnp.where(row_of > column_of, 1.0, 0.0).astype(BF16)

    def summed(values, triangle):
        high, middle, low = split3(values)
        return nn(high, triangle) + nn(middle, triangle) + nn(low, triangle)

    def offsets(values, reverse):
        totals = jnp.sum(values, axis=1, keepdims=True)
        kept = [jnp.zeros((1, 1), F32)]
        order = range(rows - 1, 0, -1) if reverse else range(rows - 1)
        for r in order:
            kept.append(kept[-1] + totals[r : r + 1])
        return jnp.concatenate(kept[::-1] if reverse else kept, axis=0)

    optical = softplus(channel[0]) * (1.0 / length)
    before = summed(optical, upper) + offsets(optical, False)
    through = jnp.exp(-before)
    decay = jnp.exp(-optical)
    weights = through * one_minus_exp(optical, decay)
    pull = []
    predictions = []
    lifted = jnp.zeros((rows, pair), F32)
    for c in range(channels_out - 1):
        signal = channel[c + 1]
        predicted = jnp.sum(
            jnp.sum(weights * signal, axis=1, keepdims=True), axis=0, keepdims=True
        )
        predictions.append(predicted)
        miss = loss_scale * (predicted - targets_ref[0, c])
        pull.append(miss * weights)
        lifted = lifted + miss * signal
    packed_ref[0:8] = jnp.concatenate(
        [jnp.zeros((8, 1), F32) + p for p in predictions]
        + [jnp.zeros((8, hidden - len(predictions)), F32)],
        axis=1,
    )
    product = lifted * weights
    after = summed(product, lower) + offsets(product, True)
    density_grad = (
        (lifted * through * decay - after) * (1.0 / length) / (1.0 + jnp.exp(-channel[0]))
    )
    grads = [density_grad] + pull
    grad_pairs = []
    for p in range(rows):
        rows4 = jnp.concatenate([g[p : p + 1] for g in grads], axis=0)
        grad_pairs.append(jnp.concatenate([rows4] * (8 // channels_out), axis=0))
    grad_swapped = [
        jnp.concatenate([piece[:, length:], piece[:, :length]], axis=1) for piece in grad_pairs
    ]
    for e in range(owners):
        halves = []
        for c in range(CAP):
            total = jnp.zeros((8, pair), F32)
            for k in range(blocks):
                source = grad_pairs if k % CAP == c else grad_swapped
                total = total + picks[k][e][c] * source[k // CAP]
            halves.append(total)
        tile = jnp.where(lane < length, halves[0], halves[1])
        sg[e] = jnp.concatenate([tile, tile], axis=0).astype(BF16)
    rg[0, 0] = sg[0]
    arriving = [[] for _ in range(groups)]
    for d in range(groups):
        for e in range(owners):
            if d or e:
                copy = pltpu.make_async_remote_copy(
                    src_ref=sg.at[e],
                    dst_ref=rg.at[d, e],
                    send_sem=sg_send.at[d, e],
                    recv_sem=sg_recv.at[d, e],
                    device_id=device(e, d),
                    device_id_type=MESH,
                )
                copy.start()
                arriving[d].append(copy)
                started.append(copy)

    for d in range(EARLY, groups):
        relays[d - 1].wait_recv()
        forward(d)

    mine = pl.ds(pl.multiple_of(my_group * share, share), share)
    gf = jnp.zeros((bricks * share, hidden), F32)
    gs = jnp.zeros((bricks * share, hidden), F32)
    go = jnp.zeros((bricks * channels_out, share), F32)
    for d in range(groups):
        mask = masks(d)
        for copy in arriving[d]:
            copy.wait_recv()
        rows16 = jnp.concatenate([rg[d, e] for e in range(owners)], axis=1)
        rows16 = rows16 * jnp.where(label_tile(d) == brick_row, 1.0, 0.0).astype(BF16)
        d2 = (nn(wo_t, rows16) * slope2_s[d]).astype(BF16)
        d1 = (nn(w2_cat, masked(d2, mask)) * slope1_s[d]).astype(BF16)
        gs = gs + nt(masked(h1_s[d, mine, :], mask), d2)
        go = go + nt(rows16, h2_s[d, mine, :])
        gf = gf + nt(masked(enc_s[d, mine, :], mask), d1)
    at = 8
    for block in (
        jnp.concatenate([go, jnp.zeros((go.shape[0], hidden - share), F32)], axis=1),
        gf,
        gs,
    ):
        packed_ref[at : at + block.shape[0]] = block
        at = at + block.shape[0]

    for copy in started:
        copy.wait_send()


def fused_plan(samples, frequencies, w_first, w_second, w_out, brick_ids, targets):
    owners = lax.axis_size("brick")
    rays = lax.axis_size("ray")
    reps = lax.axis_size("rep")
    groups = rays * reps
    bricks, features, hidden = w_first.shape
    out = w_out.shape[1]
    length = samples.shape[3]
    pair = CAP * length
    wide = owners * pair
    share = features // groups
    vmem = pl.BlockSpec(memory_space=pltpu.VMEM)
    smem = pl.BlockSpec(memory_space=pltpu.SMEM)
    hbm = pl.BlockSpec(memory_space=pltpu.MemorySpace.HBM)
    dma = pltpu.SemaphoreType.DMA
    packed = pl.pallas_call(
        functools.partial(fused_kernel, owners, rays, reps),
        out_shape=jax.ShapeDtypeStruct((8 + bricks * (out + 2 * share), hidden), F32),
        in_specs=[smem, smem, hbm, hbm, hbm, hbm, hbm],
        out_specs=vmem,
        scratch_shapes=[
            pltpu.VMEM((owners, 32, pair), BF16),
            pltpu.VMEM((groups, owners, 32, pair), BF16),
            pltpu.VMEM((owners, 8, pair), F32),
            pltpu.VMEM((owners, 8, pair), F32),
            pltpu.VMEM((owners, 16, pair), BF16),
            pltpu.VMEM((groups, owners, 16, pair), BF16),
            pltpu.VMEM(samples.shape, BF16),
            pltpu.VMEM(frequencies.shape, F32),
            pltpu.VMEM(w_first.shape, BF16),
            pltpu.VMEM(w_second.shape, BF16),
            pltpu.VMEM(w_out.shape, BF16),
            pltpu.VMEM((groups, features, wide), BF16),
            pltpu.VMEM((groups, hidden, wide), BF16),
            pltpu.VMEM((groups, hidden, wide), BF16),
            pltpu.VMEM((groups, hidden, wide), F32),
            pltpu.VMEM((groups, hidden, wide), F32),
            dma((5,)),
            dma((owners,)),
            dma((owners,)),
            dma((groups,)),
            dma((groups,)),
            dma((owners,)),
            dma((owners,)),
            dma((groups, owners)),
            dma((groups, owners)),
        ],
        compiler_params=pltpu.CompilerParams(
            collective_id=0, has_side_effects=True,
            vmem_limit_bytes=63 * 1024 * 1024,
        ),
    )(brick_ids, targets.T, samples, frequencies, w_first, w_second, w_out)
    signals = targets.shape[0]
    last, first, second = 8, 8 + bricks * out, 8 + bricks * (out + share)
    return (
        packed[:1, :signals].T,
        packed[first:second].reshape(bricks, share, hidden),
        packed[second:].reshape(bricks, share, hidden),
        packed[last:first, :share].reshape(bricks, out, share),
    )


def on_device(samples, frequencies, w_first, w_second, w_out, brick_ids, targets):
    owners = lax.axis_size("brick")
    groups = lax.axis_size(("ray", "rep"))
    bricks, features, hidden = w_first.shape
    ray_rows, blocks, channels, length = samples.shape
    fits = (
        ray_rows == 1
        and blocks % CAP == 0
        and CAP == 2
        and CAP * length == 128
        and channels == 16
        and bricks * w_out.shape[1] == 16
        and features == hidden
        and features % (16 * groups) == 0
        and groups * owners <= 16
    )
    plan = fused_plan if fits else layered_plan
    return plan(samples, frequencies, w_first, w_second, w_out, brick_ids, targets)


def solution(mesh):
    return jax.shard_map(
        on_device,
        mesh=mesh,
        in_specs=(
            P(("grp", "brick", "ray", "rep"), None, None, None),
            P(),
            P("brick", None, None),
            P("brick", None, None),
            P("brick", None, None),
            P(("grp", "brick", "ray", "rep"), None),
            P(None, ("grp", "brick", "ray", "rep")),
        ),
        out_specs=(
            P(None, ("grp", "brick", "ray", "rep")),
            P(("grp", "brick"), ("ray", "rep"), None),
            P(("grp", "brick"), ("ray", "rep"), None),
            P(("grp", "brick"), None, ("ray", "rep")),
        ),
        check_vma=False,
    )
```
